512 devices in a mesh: lat: 64 (over y, z_hi, core), lon: 8 (over x, z_lo).
Axes of the slice: x: 4, y: 8, z: 8 (z_hi: 4, z_lo: 2; z = z_hi * 2 + z_lo), core: 2. Of those that a mesh axis runs over, the one named last changes fastest.
Arguments:
- tracers: float32 [16, 6, 256, 2048], P(None, None, 'lat', 'lon'), may hold values from -6 to 6
- velocity: float32 [2, 256, 2048], P(None, 'lat', 'lon'), may hold values from -4 to 4
- stress: float32 [3, 256, 2048], P(None, 'lat', 'lon'), may hold values from -6 to 6
- strength: float32 [256, 2048], P('lat', 'lon'), may hold values from 0.5 to 5
- inverse_mass: float32 [256, 2048], P('lat', 'lon'), may hold values from 0.2 to 2
- wind: float32 [2, 256, 2048], P(None, 'lat', 'lon'), may hold values from -4 to 4
- ocean_mask: int32 [256, 2048], P('lat', 'lon'), may hold values 0 or 1
Outputs:
- new_velocity: float32 [2, 256, 2048], P(None, 'lat', 'lon')
- new_stress: float32 [3, 256, 2048], P(None, 'lat', 'lon')
- new_tracers: float32 [16, 6, 256, 2048], P(None, None, 'lat', 'lon')
The draws below stay inside these ranges and needn't reach their ends.
All inputs are finite; a program needn't handle non-finite values. No bound on the sum of `ocean_mask` on one device may be relied on, other than what follows from the above.
Results may differ from the reference program's by a relative error of at most 0.00007.
Values sent between devices are 32-bit elements; how exact they have to be, the bound alone decides.
A program may use at most 64 MiB of HBM per device.

```python
import math
import jax
import jax.numpy as jnp
import numpy as np
from jax import lax

NTR = 16
ITERS = 2
NX = 256
NY = 2048


def touch_ends(values, rng, smallest, top_value):
    dims = values.shape
    index_at = [jax.random.randint(jax.random.fold_in(rng, axis), (), 0, dims[axis]) for axis in range(len(dims))]
    values = values.at[tuple(index_at)].set(smallest)
    longest = dims.index(max(dims))
    index_at[longest] = (index_at[longest] + 1) % dims[longest]
    return values.at[tuple(index_at)].set(top_value)


def shard_levels(stream_key, extent, pieces, low, largest):
    level = 1.0
    for axis_at, blocks in pieces:
        steps = jax.random.uniform(jax.random.fold_in(jax.random.fold_in(stream_key, 6), axis_at), (blocks,), jnp.float32, low / len(pieces), largest / len(pieces))
        level = level * jnp.repeat(jnp.exp(steps), extent[axis_at] // blocks).reshape((-1,) + (1,) * (len(extent) - 1 - axis_at))
    return level


def normal_values(rng, extent, width, most, pieces=(), kind=jnp.bfloat16):
    entries = width * jax.random.normal(rng, extent, jnp.float32)
    if pieces:
        entries = entries * shard_levels(rng, extent, pieces, -0.22, 0.18)
    return jnp.clip(entries, -most, most).astype(kind)


def setup_inputs(seed: int = 0) -> dict:
    key_list = jax.random.split(jax.random.key(seed), 8)
    return {
        "tracers": normal_values(key_list[0], (NTR, 6, NX, NY), 1.0, 6.0, ((2, 64), (3, 8)), jnp.float32),
        "velocity": normal_values(key_list[1], (2, NX, NY), 0.3, 4.0, ((1, 64), (2, 8)), jnp.float32),
        "stress": normal_values(key_list[2], (3, NX, NY), 1.0, 6.0, ((1, 64), (2, 8)), jnp.float32),
        "strength": jnp.clip(jnp.exp(math.log(5.0) - 2.3025851 * jax.random.uniform(key_list[3], (NX, NY), jnp.float32) ** shard_levels(key_list[3], (NX, NY), ((0, 64), (1, 8)), -0.2, 0.2)), 0.5, 5.0),
        "inverse_mass": jnp.clip(jnp.exp(math.log(2.0) - 2.3025851 * jax.random.uniform(key_list[4], (NX, NY), jnp.float32) ** shard_levels(key_list[4], (NX, NY), ((0, 64), (1, 8)), -0.2, 0.2)), 0.2, 2.0),
        "wind": normal_values(key_list[5], (2, NX, NY), 0.5, 4.0, ((1, 64), (2, 8)), jnp.float32),
        "ocean_mask": touch_ends((jax.random.randint(key_list[6], (NX, NY), 0, 5) < 4).astype(jnp.int32), jax.random.fold_in(key_list[6], 1), 0, 1),
    }


ellipse_inv = 0.25
floor_rate = 0.1
relax_stress = 3.0
relax_velocity = 3.0
drag_rate = 1.0
time_step = 0.15

def basis_values(xi, eta):
    return [1.0, xi, eta, 1.5 * xi * xi - 0.5, xi * eta, 1.5 * eta * eta - 0.5]

def quad_tables():
    root = math.sqrt(0.6)
    gauss = [-root, 0.0, root]
    weights = [5.0 / 9.0, 8.0 / 9.0, 5.0 / 9.0]
    points = [(gauss[a], gauss[b], weights[a] * weights[b]) for b in range(3) for a in range(3)]
    volume = np.array([basis_values(x, e) for x, e, w in points])
    slope_xi = np.array([[0.0, w, 0.0, 3.0 * x * w, e * w, 0.0] for x, e, w in points])
    slope_eta = np.array([[0.0, 0.0, w, 0.0, x * w, 3.0 * e * w] for x, e, w in points])
    shape = np.array([[(1 - x) * (1 - e) / 4, (1 + x) * (1 - e) / 4, (1 - x) * (1 + e) / 4, (1 + x) * (1 + e) / 4] for x, e, w in points])
    north = np.array([basis_values(s, 1.0) for s in gauss])
    south = np.array([basis_values(s, -1.0) for s in gauss])
    east = np.array([basis_values(1.0, s) for s in gauss])
    west = np.array([basis_values(-1.0, s) for s in gauss])
    wcol = np.array(weights)[:, None]
    gcol = np.array(gauss)
    return {'volume': volume, 'slope_xi': slope_xi, 'slope_eta': slope_eta, 'shape': shape, 'faces': np.concatenate([north, south, east, west], 0), 'north_w': wcol * north, 'south_w': wcol * south, 'east_w': wcol * east, 'west_w': wcol * west, 'half_low': (1 - gcol) / 2, 'half_high': (1 + gcol) / 2, 'inv_mass': 1.0 / np.array([4.0, 4.0 / 3.0, 4.0 / 3.0, 0.8, 4.0 / 9.0, 0.8])}

def table(tabs, name):
    return jnp.asarray(tabs[name], jnp.float32)

def contract(form, left, right):
    return jnp.einsum(form, left, right, precision=lax.Precision.HIGHEST)

def face_traces(coefs, tabs):
    every = contract('fk,rkxy->rfxy', table(tabs, 'faces'), coefs)
    return (every[:, 0:3], every[:, 3:6], every[:, 6:9], every[:, 9:12])

def dg_rate(coefs, traces, ocean, uext, rims, row_factor, tabs):
    north, south, east, west = traces
    low_row, low_row_mask, high_row, high_row_mask, low_col, low_col_mask, high_col, high_col_mask = rims
    half_low = table(tabs, 'half_low')[:, None, None]
    half_high = table(tabs, 'half_high')[:, None, None]
    lower = jnp.concatenate([low_row[:, :, None, :], north], 2)
    upper = jnp.concatenate([south, high_row[:, :, None, :]], 2)
    row_active = jnp.concatenate([low_row_mask[None], ocean], 0) * jnp.concatenate([ocean, high_row_mask[None]], 0) * row_factor[:, None]
    normal_row = half_low * uext[1][None, :, :-1] + half_high * uext[1][None, :, 1:]
    row_flux = (jnp.maximum(normal_row, 0.0) * lower + jnp.minimum(normal_row, 0.0) * upper) * row_active
    row_part = contract('sm,rsxy->rmxy', table(tabs, 'south_w'), row_flux[:, :, :-1]) - contract('sm,rsxy->rmxy', table(tabs, 'north_w'), row_flux[:, :, 1:])
    left = jnp.concatenate([low_col[:, :, :, None], east], 3)
    right = jnp.concatenate([west, high_col[:, :, :, None]], 3)
    col_active = jnp.concatenate([low_col_mask[:, None], ocean], 1) * jnp.concatenate([ocean, high_col_mask[:, None]], 1)
    normal_col = half_low * uext[0][None, :-1, :] + half_high * uext[0][None, 1:, :]
    col_flux = (jnp.maximum(normal_col, 0.0) * left + jnp.minimum(normal_col, 0.0) * right) * col_active
    col_part = contract('sm,rsxy->rmxy', table(tabs, 'west_w'), col_flux[..., :-1]) - contract('sm,rsxy->rmxy', table(tabs, 'east_w'), col_flux[..., 1:])
    corners = jnp.stack([uext[:, :-1, :-1], uext[:, :-1, 1:], uext[:, 1:, :-1], uext[:, 1:, 1:]], 1)
    at_points = contract('pa,caxy->cpxy', table(tabs, 'shape'), corners)
    values = contract('pk,rkxy->rpxy', table(tabs, 'volume'), coefs)
    volume = contract('pm,rpxy->rmxy', table(tabs, 'slope_xi'), values * at_points[0]) + contract('pm,rpxy->rmxy', table(tabs, 'slope_eta'), values * at_points[1])
    return (volume + row_part + col_part) * table(tabs, 'inv_mass')[None, :, None, None] * ocean

def stress_forces(current, uext, strength, ocean):
    c00 = uext[:, :-1, :-1]
    c10 = uext[:, :-1, 1:]
    c01 = uext[:, 1:, :-1]
    c11 = uext[:, 1:, 1:]
    along_x = 0.5 * (c10 + c11 - c00 - c01)
    along_y = 0.5 * (c01 + c11 - c00 - c10)
    strain_xx = along_x[0]
    strain_yy = along_y[1]
    strain_xy = 0.5 * (along_y[0] + along_x[1])
    delta = jnp.sqrt((strain_xx * strain_xx + strain_yy * strain_yy) * (1.0 + ellipse_inv) + 4.0 * ellipse_inv * strain_xy * strain_xy + 2.0 * strain_xx * strain_yy * (1.0 - ellipse_inv) + floor_rate * floor_rate)
    zeta = strength / (2.0 * delta)
    shear = zeta * ellipse_inv
    trace_rate = strain_xx + strain_yy
    plastic = jnp.stack([2.0 * shear * strain_xx + (zeta - shear) * trace_rate - 0.5 * strength, 2.0 * shear * strain_yy + (zeta - shear) * trace_rate - 0.5 * strength, 2.0 * shear * strain_xy], 0)
    current = ocean * (current + (plastic - current) / relax_stress)
    forces = []
    for sign_x, sign_y in ((-1.0, -1.0), (1.0, -1.0), (-1.0, 1.0), (1.0, 1.0)):
        force_x = -0.5 * (current[0] * sign_x + current[2] * sign_y)
        force_y = -0.5 * (current[2] * sign_x + current[1] * sign_y)
        forces.append(jnp.stack([force_x, force_y], 0))
    return (current, jnp.stack(forces, 1))

def spread_corners(terms):
    return jnp.pad(terms[:, 0], ((0, 0), (0, 1), (0, 1))) + jnp.pad(terms[:, 1], ((0, 0), (0, 1), (1, 0))) + jnp.pad(terms[:, 2], ((0, 0), (1, 0), (0, 1))) + jnp.pad(terms[:, 3], ((0, 0), (1, 0), (1, 0)))

def update_velocity(moving, velocity, inverse_mass, force, wind, active):
    return active * (relax_velocity * moving + velocity + inverse_mass * (force + wind)) / (1.0 + relax_velocity + inverse_mass * drag_rate)

def node_corners(moving):
    ext = jnp.concatenate([moving, jnp.zeros_like(moving[:, :1])], 1)
    return jnp.concatenate([ext, ext[:, :, :1]], 2)

def assemble(terms):
    grid = spread_corners(terms)
    folded = jnp.concatenate([grid[:, :, 0:1] + grid[:, :, -1:], grid[:, :, 1:-1]], 2)
    return folded[:, :-1]

def reference(tracers, velocity, stress, strength, inverse_mass, wind, ocean_mask):
    tabs = quad_tables()
    ocean = ocean_mask.astype(jnp.float32)
    count = assemble(jnp.broadcast_to(ocean, (1, 4) + ocean.shape))
    row_mask = (jnp.arange(NX) > 0).astype(jnp.float32)[:, None]
    active = jnp.minimum(count[0], 1.0) * row_mask
    moving = velocity
    current = stress
    for turn in range(ITERS):
        current, forces = stress_forces(current, node_corners(moving), strength, ocean)
        moving = update_velocity(moving, velocity, inverse_mass, assemble(forces), wind, active)
    uext = node_corners(moving)
    row_factor = jnp.ones((NX + 1,), jnp.float32)

    def rate_block(coefs):
        traces = face_traces(coefs, tabs)
        count_tr = coefs.shape[0]
        zero_row = jnp.zeros((count_tr, 3, NY), jnp.float32)
        zero_mask = jnp.zeros((NY,), jnp.float32)
        rims = (zero_row, zero_mask, zero_row, zero_mask, traces[2][:, :, :, -1], ocean[:, -1], traces[3][:, :, :, 0], ocean[:, 0])
        return dg_rate(coefs, traces, ocean, uext, rims, row_factor, tabs)

    def rate(coefs):
        blocks = coefs.reshape((4, NTR // 4) + coefs.shape[1:])
        return lax.map(rate_block, blocks).reshape(coefs.shape)
    first = tracers + time_step * rate(tracers)
    second = 0.75 * tracers + 0.25 * (first + time_step * rate(first))
    third = tracers / 3.0 + 2.0 / 3.0 * (second + time_step * rate(second))
    return (moving, current, ocean * third)
```

```python
import functools
import math

import jax
import jax.numpy as jnp
from jax import lax
from jax.experimental import pallas as pl
from jax.experimental.pallas import tpu as pltpu
from jax.sharding import PartitionSpec as P

MESH = pl.DeviceIdType.MESH
F32 = jnp.float32
NTR, ROWS, COLS = 16, 4, 256
ITERS = 2
GAUSS = math.sqrt(0.6)
DT = 0.15
THIRD = 1.0 / 3.0
VEL, STRESS, STRENGTH, MASS, WIND, OCEAN, FIELDS = 0, 2, 5, 6, 7, 9, 10
VOL, NORTH, EAST, LAND, COEFS = 0, 24, 27, 30, 31
SLOT = (0, 8, 64, 72)
AROUND = ((0, -1), (0, 1), (-1, 0), (1, 0), (-1, -1), (-1, 1), (1, -1), (1, 1))


def lanes(shape):
    return lax.broadcasted_iota(jnp.int32, shape, len(shape) - 1)


def sublanes(shape):
    return lax.broadcasted_iota(jnp.int32, shape, len(shape) - 2)


def turn(x, by, axis):
    by = by % x.shape[axis] if isinstance(by, int) else by
    return x if isinstance(by, int) and by == 0 else pltpu.roll(x, by, axis)


def line_traces(a, b, mid, along, across, cross):
    base = a + b
    outer = base + 0.4 * mid
    inner = base - 0.5 * mid
    slope_high = along + cross
    slope_low = along - cross
    high = outer + across
    low = outer - across
    return (
        (high - slope_high, inner + across, high + slope_high),
        (low - slope_low, inner - across, low + slope_low),
    )


def row_traces(c):
    return line_traces(c[0], c[5], c[3], GAUSS * c[1], c[2], GAUSS * c[4])


def col_traces(c):
    return line_traces(c[0], c[3], c[5], GAUSS * c[2], c[1], GAUSS * c[4])


def face_moments(weights, inside, outside):
    f = [w * jnp.where(w > 0.0, a, b) for w, a, b in zip(weights, inside, outside)]
    both = f[0] + f[2]
    return (both + f[1], f[2] - f[0], 0.4 * both - 0.5 * f[1])


def rate(c, k, north, south, east, west):
    d_row = [s - n for s, n in zip(south, north)]
    d_col = [w - e for w, e in zip(west, east)]
    sum_row = [south[i] + north[i] for i in range(2)]
    sum_col = [west[i] + east[i] for i in range(2)]
    g0 = d_row[0] + d_col[0]
    g1 = k(0) * c[0] + k(1) * c[1] + k(2) * c[2] + k(3) * c[4] + (3.0 * GAUSS) * d_row[1] - 3.0 * sum_col[0]
    g2 = k(4) * c[0] + k(5) * c[1] + k(6) * c[2] + k(7) * c[4] + (3.0 * GAUSS) * d_col[1] - 3.0 * sum_row[0]
    g3 = k(8) * c[1] + k(9) * c[0] + k(10) * c[3] + k(11) * c[4] + k(12) * c[2] + 5.0 * (d_row[2] + d_col[0])
    g5 = k(13) * c[2] + k(14) * c[0] + k(15) * c[5] + k(16) * c[4] + k(17) * c[1] + 5.0 * (d_row[0] + d_col[2])
    g4 = (
        k(18) * c[0] + k(19) * c[1] + k(20) * c[2] + k(21) * c[3] + k(22) * c[4] + k(23) * c[5]
        - (9.0 * GAUSS) * (sum_row[1] + sum_col[1])
    )
    return (g0, g1, g2, g3, g4, g5)


def kernel(
    nlat, nlon,
    tr, vel, stress, strength, mass, wind, mask,
    o_vel, o_str, o_tr,
    raw, mp, mski, mps, mpn, vn2, ep, lep, q, lq, c0, ts, tn, tup, tdown, c1, c2, kf, ks, st, st1, sx, fl,
    lsem, ssem, rsem,
):
    lat = lax.axis_index("lat")
    lon = lax.axis_index("lon")
    east = lax.rem(lon + 1, nlon)
    west = lax.rem(lon + nlon - 1, nlon)
    has = {1: lat < nlat - 1, -1: lat > 0, -2: lat > 1, 2: lat < nlat - 2}

    def device(dlat, dlon):
        return (lat + dlat, {0: lon, 1: east, -1: west}[dlon])

    def given(dlat, act):
        if dlat == 0:
            act()
        else:
            pl.when(has[dlat])(act)

    local = [
        pltpu.make_async_copy(src, dst, lsem.at[i])
        for i, (src, dst) in enumerate(
            [
                (vel, mp.at[pl.ds(VEL, 2)]),
                (stress, mp.at[pl.ds(STRESS, 3)]),
                (strength, mp.at[STRENGTH]),
                (mass, mp.at[MASS]),
                (wind, mp.at[pl.ds(WIND, 2)]),
                (mask, mski),
                (tr.at[pl.ds(0, 384)], raw.at[pl.ds(0, 384)]),
                (tr.at[pl.ds(384, 384)], raw.at[pl.ds(384, 384)]),
            ]
        )
    ]

    barrier = pltpu.get_barrier_semaphore()

    def greet(dlat):
        for dlon in (0, 1, -1):
            if dlat or dlon:
                pl.semaphore_signal(barrier, inc=1, device_id=device(dlat, dlon), device_id_type=MESH)

    for dlat in (1, 0, -1, 2):
        given(dlat, functools.partial(greet, dlat))
    for copy in local:
        copy.start()

    table = []

    def message(src, dst, dlat, dlon):
        i = len(table)
        table.append((
            dlat,
            pltpu.make_async_remote_copy(
                src_ref=src, dst_ref=dst, send_sem=ssem.at[i], recv_sem=rsem.at[i],
                device_id=device(dlat, dlon), device_id_type=MESH,
            ),
        ))
        return i

    first = []
    for dlat in (1, -1, 0, -2):
        for dlon in (1, -1):
            first.append(message(ep, lep.at[0 if dlon < 0 else 1, {1: 0, 0: 1, -1: 2, -2: 3}[dlat]], dlat, dlon))
    first.append(message(mp, mps, 1, 0))
    first.append(message(mp, mpn, -1, 0))
    first.append(message(mp.at[pl.ds(VEL, 2)], vn2, -2, 0))
    edges = [message(q, lq.at[AROUND.index((-dlat, -dlon))], dlat, dlon) for dlat, dlon in AROUND]
    bulk = []
    for g in range(2):
        bulk.append([
            message(c0.at[g, pl.ds(4, 2)], c0.at[g, pl.ds(0, 2)], 1, 0),
            message(c0.at[g, pl.ds(2, 2)], c0.at[g, pl.ds(6, 2)], -1, 0),
            message(tup.at[g], ts.at[g], 1, 0),
            message(tdown.at[g], tn.at[g], -1, 0),
        ])

    def send(some):
        for dlat in (1, -1, 0, -2):
            mine = [i for i in some if table[i][0] == dlat]
            if mine:
                given(dlat, lambda mine=mine: [table[i][1].start() for i in mine] and None)

    def arrive(some):
        for dlat in (0, 1, -1, -2):
            mine = [i for i in some if table[i][0] == dlat]
            if mine:
                given(-dlat, lambda mine=mine: [table[i][1].wait_recv() for i in mine] and None)

    def sent(some):
        for dlat in (0, 1, -1, -2):
            mine = [i for i in some if table[i][0] == dlat]
            if mine:
                given(dlat, lambda mine=mine: [table[i][1].wait_send() for i in mine] and None)

    def clear(row, trace, steps):
        for g in range(2):
            for i in (row, row + 1):
                for k in range(6):
                    c0[g, i, k] = jnp.zeros((8, COLS), F32)
            for i in range(3):
                trace[g, i] = jnp.zeros((8, COLS), F32)
        for n, (dlat, _) in enumerate(AROUND):
            if dlat == steps:
                for m in range(3):
                    lq[n, m] = jnp.zeros((8, 128), F32)

    pl.when(lat == 0)(lambda: clear(0, ts, -1))
    pl.when(lat == nlat - 1)(lambda: clear(6, tn, 1))

    for copy in local[:6]:
        copy.wait()
    mp[OCEAN] = mski[...].astype(F32)
    at4 = lanes((4, 128))
    for h in range(2):
        acc = jnp.zeros((4, 128), F32)
        for f in range(8 * h, min(8 * h + 8, FIELDS)):
            p = 16 * (f % 8)
            x = mp[f]
            acc = jnp.where((at4 >= p) & (at4 < p + 8), turn(x[:, :128], p, 1), acc)
            acc = jnp.where((at4 >= p + 8) & (at4 < p + 16), turn(x[:, 128:], p + 16, 1), acc)
        ep[h] = acc

    one = jnp.int32(1)
    zero = jnp.int32(0)
    targets = 2 + 3 * (jnp.where(has[1], one, zero) + jnp.where(has[-1], one, zero) + jnp.where(has[-2], one, zero))
    pl.semaphore_wait(barrier, targets)
    send(first)

    def lay_out(g):
        def row(i, _):
            for k in range(6):
                for t in range(2):
                    c0[g, i + 2, k, :, t * 128:(t + 1) * 128] = raw[pl.ds(g * 384 + k * 8 + t * 4 + i, 8, stride=48), :]
            return 0

        lax.fori_loop(0, ROWS, row, 0)
        for i in range(3):
            pass
        up = row_traces([c0[g, 3, k] for k in range(6)])[0]
        down = row_traces([c0[g, 4, k] for k in range(6)])[1]
        for i in range(3):
            tup[g, i] = up[i]
            tdown[g, i] = down[i]

    at8 = lanes((8, 128))
    in_row = at8 % 16

    def pack_edges(m, _):
        acc = None
        for j in range(4):
            s = 4 * m + j
            g, k = s // 6, s % 6
            strip = jnp.zeros((8, 128), F32)
            for i in range(ROWS):
                x = c0[g, i + 2, k]
                x = jnp.where(at8 < 4, x[:, :128], turn(x[:, 128:], 8, 1))
                p = 16 * (i + 2) + 4
                strip = jnp.where((at8 >= p) & (at8 < p + 8), turn(x, p, 1), strip)
            st[s] = strip
            acc = strip if acc is None else acc + turn(strip, SLOT[j], 1)
        q[m] = acc
        return 0

    local[6].wait()
    lay_out(0)
    send(bulk[0])
    local[7].wait()
    lay_out(1)
    lax.fori_loop(0, 3, pack_edges, 0)
    send(edges)
    send(bulk[1])

    arrive(first)
    wide = (16, 384)
    grow = 4 * lat - 4 + sublanes(wide)
    inside = (grow >= 0) & (grow < 4 * nlat)
    packed = [[jnp.concatenate([lep[s, r, h] for r in range(4)], 0) for h in range(2)] for s in range(2)]
    at16 = lanes((16, 128))

    def extended(f):
        h, p = f // 8, 16 * (f % 8)
        north2 = vn2[f - VEL] if f < VEL + 2 else jnp.zeros((4, COLS), F32)
        here = jnp.concatenate([mps[f], mp[f], mpn[f], north2], 0)
        side = jnp.where(at16 < 64, turn(packed[0][h], -p, 1), turn(packed[1][h], 112 - p, 1))
        return jnp.where(inside, jnp.concatenate([here, side], 1), 0.0)

    def above(x):
        return turn(x, -1, 0)

    def below(x):
        return turn(x, 1, 0)

    def right(x):
        return turn(x, -1, 1)

    def left(x):
        return turn(x, 1, 1)

    f = [extended(i) for i in range(FIELDS)]
    start = f[VEL:VEL + 2]
    moving = f[VEL:VEL + 2]
    current = f[STRESS:STRESS + 3]
    power, weight, push, ocean = f[STRENGTH], f[MASS], f[WIND:WIND + 2], f[OCEAN]
    count = ocean + below(ocean)
    count = count + left(count)
    active = jnp.where((grow > 0) & (grow < 4 * nlat), jnp.minimum(count, 1.0), 0.0)
    scale = active / (4.0 + weight)
    fixed = [start[i] + weight * push[i] for i in range(2)]

    def slopes(x):
        total, diff = x + above(x), above(x) - x
        return 0.5 * (right(total) - total), 0.5 * (diff + right(diff))

    def force(along, across):
        p = along + below(along)
        r = across - below(across)
        return 0.5 * ((p - left(p)) + (r + left(r)))

    for _ in range(ITERS):
        e11, ux_y = slopes(moving[0])
        uy_x, e22 = slopes(moving[1])
        e12 = 0.5 * (ux_y + uy_x)
        inner = (e11 * e11 + e22 * e22) * 1.25 + e12 * e12 + 1.5 * e11 * e22 + 0.01
        zeta = 0.5 * power / jnp.sqrt(inner)
        shear = 0.25 * zeta
        spread = (zeta - shear) * (e11 + e22) - 0.5 * power
        plastic = (2.0 * shear * e11 + spread, 2.0 * shear * e22 + spread, 2.0 * shear * e12)
        current = [ocean * (a + (b - a) * THIRD) for a, b in zip(current, plastic)]
        s11, s22, s12 = current
        pushed = (force(s11, s12), force(s12, s22))
        moving = [scale * (3.0 * moving[i] + fixed[i] + weight * pushed[i]) for i in range(2)]

    for i in range(2):
        o_vel[i] = moving[i][4:8, :COLS]
    for i in range(3):
        o_str[i] = current[i][4:8, :COLS]

    def modes(x):
        total, diff = x + above(x), above(x) - x
        rt, rd = right(total), right(diff)
        w = (0.25 * DT) * ocean
        return w * (total + rt), w * (rt - total), w * (diff + rd), w * (rd - diff)

    def normals(a, b, act):
        mean, half = 0.5 * (a + b), (0.5 * GAUSS) * (b - a)
        return ((5.0 / 9.0) * act * (mean - half), (8.0 / 9.0) * act * mean, (5.0 / 9.0) * act * (mean + half))

    u0, u1, u2, u3 = modes(moving[0])
    v0, v1, v2, v3 = modes(moving[1])
    vn = above(moving[1])
    ue = right(moving[0])
    coefs = [
        3.0 * u0, u1, u2, THIRD * u3,
        3.0 * v0, v1, v2, THIRD * v3,
        5.0 * u0, 5.0 * u1, 2.0 * u1, (5.0 * THIRD) * u2, (5.0 * THIRD) * u3,
        5.0 * v0, 5.0 * v2, 2.0 * v2, (5.0 * THIRD) * v1, (5.0 * THIRD) * v3,
        3.0 * (u2 + v1), 3.0 * v0 + u3, 3.0 * u0 + v3, 1.2 * v1, u1 + v2, 1.2 * u2,
    ]
    coefs += normals(vn, right(vn), (0.25 * DT) * ocean * above(ocean))
    coefs += normals(ue, above(ue), (0.25 * DT) * ocean * right(ocean))
    coefs.append(ocean)
    own_lanes = (at8 // 16) == sublanes((8, 128))
    for i, x in enumerate(coefs):
        kf[i] = x[:, :COLS]
        if i < LAND:
            a, b, c = x[:, :128], x[:, 128:256], x[:, 256:]
            low = turn(jnp.where(at16 >= 124, c, a), 4, 1)
            high = turn(jnp.where(at16 >= 124, b, c), 12, 1)
            z = turn(jnp.where(at16 < 8, low, high), -2, 0)[:8]
            z = jnp.where(own_lanes, pltpu.roll(z, 0, 1, stride=16, stride_axis=0), 0.0)
            for by in (4, 2, 1):
                z = z + turn(z, by, 0)
            ks[i] = z

    arrive(edges)

    def unpack_edges(m, _):
        for j in range(4):
            s = 4 * m + j
            strip = st[s]
            for n, (dlat, dlon) in enumerate(AROUND):
                by = -SLOT[j] + 8 * dlon + 64 * dlat
                ok = {-1: in_row < 4, 0: (in_row >= 4) & (in_row < 12), 1: in_row >= 12}[dlon]
                ok = ok & {-1: at8 < 32, 0: (at8 >= 32) & (at8 < 96), 1: at8 >= 96}[dlat]
                strip = jnp.where(ok, turn(lq[n, m], by, 1), strip)
            st[s] = strip
        return 0

    lax.fori_loop(0, 3, unpack_edges, 0)

    def strip_columns(c):
        e, w = col_traces(c)
        return face_moments([ks[EAST + i] for i in range(3)], e, [turn(x, -1, 1) for x in w])

    def strip_rate(c):
        n, s = row_traces(c)
        north = face_moments([ks[NORTH + i] for i in range(3)], n, [turn(x, -16, 1) for x in s])
        east_m = strip_columns(c)
        g = rate(c, lambda i: ks[VOL + i], north, [turn(x, 16, 1) for x in north], east_m, [turn(x, 1, 1) for x in east_m])
        return g, east_m

    lane = lanes((8, COLS))

    for g in range(2):
        base = [st[6 * g + k] for k in range(6)]
        r, m = strip_rate(base)
        for i in range(3):
            sx[0, i] = m[i]
        now = [a + b for a, b in zip(base, r)]
        r, m = strip_rate(now)
        for i in range(3):
            sx[1, i] = m[i]
        now = [0.75 * a + 0.25 * (b + d) for a, b, d in zip(base, now, r)]
        m = strip_columns(now)
        for i in range(3):
            sx[2, i] = m[i]

        arrive(bulk[g])

        for step, (src, low, high) in enumerate(((c0.at[g], 0, 7), (c1, 0, 7), (c2, 1, 6))):

            def faces(i, carry, src=src):
                n, s = row_traces([src[i, k] for k in range(6)])
                w = [kf[NORTH + j, pl.ds(i + 1, 1), :] for j in range(3)]
                w = [jnp.broadcast_to(x, (8, COLS)) for x in w]
                m = face_moments(w, carry, s)
                for j in range(3):
                    fl[i, j] = m[j]
                return n

            if step == 0:
                last = lax.fori_loop(0, 8, faces, tuple(ts[g, j] for j in range(3)))
                w = [jnp.broadcast_to(kf[NORTH + j, 9:10, :], (8, COLS)) for j in range(3)]
                m = face_moments(w, last, [tn[g, j] for j in range(3)])
                for j in range(3):
                    fl[8, j] = m[j]
                rows = (0, 8)
            else:
                n, _ = row_traces([src[low, k] for k in range(6)])
                lax.fori_loop(low + 1, high + 1, faces, n)
                rows = (low + 1, high)

            def update(i, _, src=src, step=step):
                c = [src[i, k] for k in range(6)]

                def k_of(j):
                    return jnp.broadcast_to(kf[j, pl.ds(i + 2, 1), :], (8, COLS))

                e, w = col_traces(c)
                m = face_moments([k_of(EAST + j) for j in range(3)], e, [turn(x, -1, 1) for x in w])
                p = 16 * i
                em, wm = [], []
                for j in range(3):
                    rim = sx[step, j]
                    at_east = pltpu.roll(rim, lax.rem(127 - 11 - p + 256, 128), 1)
                    at_west = pltpu.roll(rim, lax.rem(256 - 3 - p, 128), 1)
                    x = jnp.where(lane == COLS - 1, jnp.concatenate([at_east, at_east], 1), m[j])
                    em.append(x)
                    wm.append(jnp.where(lane == 0, jnp.concatenate([at_west, at_west], 1), turn(x, 1, 1)))
                r = rate(c, k_of, [fl[i + 1, j] for j in range(3)], [fl[i, j] for j in range(3)], em, wm)
                if step == 0:
                    for k in range(6):
                        c1[i, k] = c[k] + r[k]
                elif step == 1:
                    for k in range(6):
                        c2[i, k] = 0.75 * c0[g, i, k] + 0.25 * (c[k] + r[k])
                else:
                    sea = k_of(LAND)
                    for k in range(6):
                        x = sea * (THIRD * c0[g, i, k] + (2.0 * THIRD) * (c[k] + r[k]))
                        for t in range(2):
                            o_tr[pl.ds(g * 384 + k * 8 + t * 4 + i - 2, 8, stride=48), :] = x[:, t * 128:(t + 1) * 128]
                return 0

            lax.fori_loop(*rows, update, 0)

    sent(first)
    sent(edges)
    for some in bulk:
        sent(some)


def local_step(nlat, nlon, tracers, velocity, stress, strength, inverse_mass, wind, ocean_mask):
    linear = tracers.reshape(NTR, 6, ROWS, 2, 128).transpose(0, 1, 3, 2, 4).reshape(768, 128)
    hbm = pl.BlockSpec(memory_space=pltpu.HBM)
    vmem = pl.BlockSpec(memory_space=pltpu.VMEM)
    messages = 8 + 3 + 8 + 8
    new_velocity, new_stress, new_tracers = pl.pallas_call(
        functools.partial(kernel, nlat, nlon),
        out_shape=(
            jax.ShapeDtypeStruct((2, ROWS, COLS), F32),
            jax.ShapeDtypeStruct((3, ROWS, COLS), F32),
            jax.ShapeDtypeStruct((768, 128), F32),
        ),
        in_specs=[hbm] * 7,
        out_specs=(vmem, vmem, vmem),
        scratch_shapes=[
            pltpu.VMEM((768, 128), F32),
            pltpu.VMEM((FIELDS, ROWS, COLS), F32),
            pltpu.VMEM((ROWS, COLS), jnp.int32),
            pltpu.VMEM((FIELDS, ROWS, COLS), F32),
            pltpu.VMEM((FIELDS, ROWS, COLS), F32),
            pltpu.VMEM((2, ROWS, COLS), F32),
            pltpu.VMEM((2, 4, 128), F32),
            pltpu.VMEM((2, 4, 2, 4, 128), F32),
            pltpu.VMEM((3, 8, 128), F32),
            pltpu.VMEM((8, 3, 8, 128), F32),
            pltpu.VMEM((2, 8, 6, 8, COLS), F32),
            pltpu.VMEM((2, 3, 8, COLS), F32),
            pltpu.VMEM((2, 3, 8, COLS), F32),
            pltpu.VMEM((2, 3, 8, COLS), F32),
            pltpu.VMEM((2, 3, 8, COLS), F32),
            pltpu.VMEM((8, 6, 8, COLS), F32),
            pltpu.VMEM((8, 6, 8, COLS), F32),
            pltpu.VMEM((COEFS, 16, COLS), F32),
            pltpu.VMEM((LAND, 8, 128), F32),
            pltpu.VMEM((12, 8, 128), F32),
            pltpu.VMEM((6, 8, 128), F32),
            pltpu.VMEM((3, 3, 8, 128), F32),
            pltpu.VMEM((9, 3, 8, COLS), F32),
            pltpu.SemaphoreType.DMA((8,)),
            pltpu.SemaphoreType.DMA((messages,)),
            pltpu.SemaphoreType.DMA((messages,)),
        ],
        compiler_params=pltpu.CompilerParams(
            collective_id=0, has_side_effects=True, vmem_limit_bytes=48 << 20
        ),
    )(linear, velocity, stress, strength, inverse_mass, wind, ocean_mask)
    new_tracers = new_tracers.reshape(NTR, 6, 2, ROWS, 128).transpose(0, 1, 3, 2, 4).reshape(NTR, 6, ROWS, COLS)
    return new_velocity, new_stress, new_tracers


def solution(mesh):
    in_specs = (
        P(None, None, "lat", "lon"),
        P(None, "lat", "lon"),
        P(None, "lat", "lon"),
        P("lat", "lon"),
        P("lat", "lon"),
        P(None, "lat", "lon"),
        P("lat", "lon"),
    )
    out_specs = (P(None, "lat", "lon"), P(None, "lat", "lon"), P(None, None, "lat", "lon"))
    step = functools.partial(local_step, mesh.shape["lat"], mesh.shape["lon"])
    return jax.shard_map(step, mesh=mesh, in_specs=in_specs, out_specs=out_specs, check_vma=False)
```

```python
import functools
import math

import jax
import jax.numpy as jnp
from jax import lax
from jax.experimental import pallas as pl
from jax.experimental.pallas import tpu as pltpu
from jax.sharding import PartitionSpec as P

MESH = pl.DeviceIdType.MESH
F32 = jnp.float32
NTR, ROWS, COLS = 16, 4, 256
ITERS = 2
GAUSS = math.sqrt(0.6)
DT = 0.15
THIRD = 1.0 / 3.0
VEL, STRESS, STRENGTH, MASS, WIND, OCEAN, FIELDS = 0, 2, 5, 6, 7, 9, 10
VOL, NORTH, EAST, LAND, COEFS = 0, 24, 27, 30, 31
SLOT = (0, 8, 64, 72)
AROUND = ((0, -1), (0, 1), (-1, 0), (1, 0), (-1, -1), (-1, 1), (1, -1), (1, 1))


def lanes(shape):
    return lax.broadcasted_iota(jnp.int32, shape, len(shape) - 1)


def sublanes(shape):
    return lax.broadcasted_iota(jnp.int32, shape, len(shape) - 2)


def turn(x, by, axis):
    by = by % x.shape[axis] if isinstance(by, int) else by
    return x if isinstance(by, int) and by == 0 else pltpu.roll(x, by, axis)


def line_traces(a, b, mid, along, across, cross):
    base = a + b
    outer = base + 0.4 * mid
    inner = base - 0.5 * mid
    slope_high = along + cross
    slope_low = along - cross
    high = outer + across
    low = outer - across
    return (
        (high - slope_high, inner + across, high + slope_high),
        (low - slope_low, inner - across, low + slope_low),
    )


def row_traces(c):
    return line_traces(c[0], c[5], c[3], GAUSS * c[1], c[2], GAUSS * c[4])


def col_traces(c):
    return line_traces(c[0], c[3], c[5], GAUSS * c[2], c[1], GAUSS * c[4])


def face_moments(weights, inside, outside):
    f = [w * jnp.where(w > 0.0, a, b) for w, a, b in zip(weights, inside, outside)]
    both = f[0] + f[2]
    return (both + f[1], f[2] - f[0], 0.4 * both - 0.5 * f[1])


def rate(c, k, north, south, east, west):
    d_row = [s - n for s, n in zip(south, north)]
    d_col = [w - e for w, e in zip(west, east)]
    sum_row = [south[i] + north[i] for i in range(2)]
    sum_col = [west[i] + east[i] for i in range(2)]
    g0 = d_row[0] + d_col[0]
    g1 = k(0) * c[0] + k(1) * c[1] + k(2) * c[2] + k(3) * c[4] + (3.0 * GAUSS) * d_row[1] - 3.0 * sum_col[0]
    g2 = k(4) * c[0] + k(5) * c[1] + k(6) * c[2] + k(7) * c[4] + (3.0 * GAUSS) * d_col[1] - 3.0 * sum_row[0]
    g3 = k(8) * c[1] + k(9) * c[0] + k(10) * c[3] + k(11) * c[4] + k(12) * c[2] + 5.0 * (d_row[2] + d_col[0])
    g5 = k(13) * c[2] + k(14) * c[0] + k(15) * c[5] + k(16) * c[4] + k(17) * c[1] + 5.0 * (d_row[0] + d_col[2])
    g4 = (
        k(18) * c[0] + k(19) * c[1] + k(20) * c[2] + k(21) * c[3] + k(22) * c[4] + k(23) * c[5]
        - (9.0 * GAUSS) * (sum_row[1] + sum_col[1])
    )
    return (g0, g1, g2, g3, g4, g5)


def kernel(
    nlat, nlon,
    tr, vel, stress, strength, mass, wind, mask,
    o_vel, o_str, o_tr,
    raw, mp, mski, mps, mpn, vn2, ep, lep, q, lq, c0, ts, tn, tup, tdown, c1, c2, kf, ks, st, sx, fl, lo,
    lsem, ssem, rsem,
):
    lat = lax.axis_index("lat")
    lon = lax.axis_index("lon")
    east = lax.rem(lon + 1, nlon)
    west = lax.rem(lon + nlon - 1, nlon)
    has = {1: lat < nlat - 1, -1: lat > 0, -2: lat > 1, 2: lat < nlat - 2}

    def device(dlat, dlon):
        return (lat + dlat, {0: lon, 1: east, -1: west}[dlon])

    def given(dlat, act):
        if dlat == 0:
            act()
        else:
            pl.when(has[dlat])(act)

    local = [
        pltpu.make_async_copy(src, dst, lsem.at[i])
        for i, (src, dst) in enumerate(
            [
                (vel, mp.at[pl.ds(VEL, 2)]),
                (stress, mp.at[pl.ds(STRESS, 3)]),
                (strength, mp.at[STRENGTH]),
                (mass, mp.at[MASS]),
                (wind, mp.at[pl.ds(WIND, 2)]),
                (mask, mski),
                (tr.at[pl.ds(0, 384)], raw.at[pl.ds(0, 384)]),
                (tr.at[pl.ds(384, 384)], raw.at[pl.ds(384, 384)]),
            ]
        )
    ]

    barrier = pltpu.get_barrier_semaphore()

    def greet(dlat):
        for dlon in (0, 1, -1):
            if dlat or dlon:
                pl.semaphore_signal(barrier, inc=1, device_id=device(dlat, dlon), device_id_type=MESH)

    for dlat in (1, 0, -1, 2):
        given(dlat, functools.partial(greet, dlat))
    for copy in local:
        copy.start()

    table = []

    def message(src, dst, dlat, dlon):
        i = len(table)
        table.append((
            dlat,
            pltpu.make_async_remote_copy(
                src_ref=src, dst_ref=dst, send_sem=ssem.at[i], recv_sem=rsem.at[i],
                device_id=device(dlat, dlon), device_id_type=MESH,
            ),
        ))
        return i

    first = []
    for dlat in (1, -1, 0, -2):
        for dlon in (1, -1):
            first.append(message(ep, lep.at[0 if dlon < 0 else 1, {1: 0, 0: 1, -1: 2, -2: 3}[dlat]], dlat, dlon))
    first.append(message(mp, mps, 1, 0))
    first.append(message(mp, mpn, -1, 0))
    first.append(message(mp.at[pl.ds(VEL, 2)], vn2, -2, 0))
    edges = [message(q, lq.at[AROUND.index((-dlat, -dlon))], dlat, dlon) for dlat, dlon in AROUND]
    north_rows = [
        message(c0.at[5], c0.at[1], 1, 0), message(c0.at[4], c0.at[0], 1, 0), message(tup, ts.at[1], 1, 0),
    ]
    south_rows = [
        message(c0.at[2], c0.at[6], -1, 0), message(c0.at[3], c0.at[7], -1, 0), message(tdown, tn, -1, 0),
    ]

    def send(some):
        for dlat in (1, -1, 0, -2):
            mine = [i for i in some if table[i][0] == dlat]
            if mine:
                given(dlat, lambda mine=mine: [table[i][1].start() for i in mine] and None)

    def arrive(some):
        for dlat in (0, 1, -1, -2):
            mine = [i for i in some if table[i][0] == dlat]
            if mine:
                given(-dlat, lambda mine=mine: [table[i][1].wait_recv() for i in mine] and None)

    def sent(some):
        for dlat in (0, 1, -1, -2):
            mine = [i for i in some if table[i][0] == dlat]
            if mine:
                given(dlat, lambda mine=mine: [table[i][1].wait_send() for i in mine] and None)

    def clear(row, trace, steps):
        for g in range(2):
            for i in (row, row + 1):
                for k in range(6):
                    c0[i, g, k] = jnp.zeros((8, COLS), F32)
            for i in range(3):
                trace[g, i] = jnp.zeros((8, COLS), F32)
        for n, (dlat, _) in enumerate(AROUND):
            if dlat == steps:
                for m in range(3):
                    lq[n, m] = jnp.zeros((8, 128), F32)

    pl.when(lat == 0)(lambda: clear(0, ts.at[1], -1))
    pl.when(lat == nlat - 1)(lambda: clear(6, tn, 1))

    for copy in local[:6]:
        copy.wait()
    mp[OCEAN] = mski[...].astype(F32)
    at4 = lanes((4, 128))
    for h in range(2):
        acc = jnp.zeros((4, 128), F32)
        for f in range(8 * h, min(8 * h + 8, FIELDS)):
            p = 16 * (f % 8)
            x = mp[f]
            acc = jnp.where((at4 >= p) & (at4 < p + 8), turn(x[:, :128], p, 1), acc)
            acc = jnp.where((at4 >= p + 8) & (at4 < p + 16), turn(x[:, 128:], p + 16, 1), acc)
        ep[h] = acc

    one = jnp.int32(1)
    zero = jnp.int32(0)
    targets = 2 + 3 * (jnp.where(has[1], one, zero) + jnp.where(has[-1], one, zero) + jnp.where(has[-2], one, zero))
    pl.semaphore_wait(barrier, targets)
    send(first)

    def lay_out(g):
        def row(i, _):
            for k in range(6):
                for t in range(2):
                    c0[i + 2, g, k, :, t * 128:(t + 1) * 128] = raw[pl.ds(g * 384 + k * 8 + t * 4 + i, 8, stride=48), :]
            return 0

        lax.fori_loop(0, ROWS, row, 0)

    at8 = lanes((8, 128))
    in_row = at8 % 16

    local[6].wait()
    lay_out(0)
    local[7].wait()
    lay_out(1)
    send([north_rows[0], south_rows[0]])
    send([north_rows[1], south_rows[1]])
    for g in range(2):
        up = row_traces([c0[3, g, k] for k in range(6)])[0]
        down = row_traces([c0[4, g, k] for k in range(6)])[1]
        for i in range(3):
            tup[g, i] = up[i]
            tdown[g, i] = down[i]
    for m in range(3):
        acc = None
        for j in range(4):
            s = 4 * m + j
            g, k = s // 6, s % 6
            strip = jnp.zeros((8, 128), F32)
            for i in range(ROWS):
                x = c0[i + 2, g, k]
                x = jnp.where(at8 < 4, x[:, :128], turn(x[:, 128:], 8, 1))
                p = 16 * (i + 2) + 4
                strip = jnp.where((at8 >= p) & (at8 < p + 8), turn(x, p, 1), strip)
            st[s] = strip
            acc = strip if acc is None else acc + turn(strip, SLOT[j], 1)
        q[m] = acc
    send(edges)
    send([north_rows[2], south_rows[2]])

    arrive(first)
    wide = (16, 384)
    grow = 4 * lat - 4 + sublanes(wide)
    inside = (grow >= 0) & (grow < 4 * nlat)
    packed = [[jnp.concatenate([lep[s, r, h] for r in range(4)], 0) for h in range(2)] for s in range(2)]
    at16 = lanes((16, 128))

    def extended(f):
        h, p = f // 8, 16 * (f % 8)
        north2 = vn2[f - VEL] if f < VEL + 2 else jnp.zeros((4, COLS), F32)
        here = jnp.concatenate([mps[f], mp[f], mpn[f], north2], 0)
        side = jnp.where(at16 < 64, turn(packed[0][h], -p, 1), turn(packed[1][h], 112 - p, 1))
        return jnp.where(inside, jnp.concatenate([here, side], 1), 0.0)

    def above(x):
        return turn(x, -1, 0)

    def below(x):
        return turn(x, 1, 0)

    def right(x):
        return turn(x, -1, 1)

    def left(x):
        return turn(x, 1, 1)

    f = [extended(i) for i in range(FIELDS)]
    start = f[VEL:VEL + 2]
    moving = f[VEL:VEL + 2]
    current = f[STRESS:STRESS + 3]
    power, weight, push, ocean = f[STRENGTH], f[MASS], f[WIND:WIND + 2], f[OCEAN]
    count = ocean + below(ocean)
    count = count + left(count)
    active = jnp.where((grow > 0) & (grow < 4 * nlat), jnp.minimum(count, 1.0), 0.0)
    scale = active / (4.0 + weight)
    fixed = [start[i] + weight * push[i] for i in range(2)]

    def slopes(x):
        total, diff = x + above(x), above(x) - x
        return 0.5 * (right(total) - total), 0.5 * (diff + right(diff))

    def force(along, across):
        p = along + below(along)
        r = across - below(across)
        return 0.5 * ((p - left(p)) + (r + left(r)))

    for _ in range(ITERS):
        e11, ux_y = slopes(moving[0])
        uy_x, e22 = slopes(moving[1])
        e12 = 0.5 * (ux_y + uy_x)
        inner = (e11 * e11 + e22 * e22) * 1.25 + e12 * e12 + 1.5 * e11 * e22 + 0.01
        zeta = 0.5 * power / jnp.sqrt(inner)
        shear = 0.25 * zeta
        spread = (zeta - shear) * (e11 + e22) - 0.5 * power
        plastic = (2.0 * shear * e11 + spread, 2.0 * shear * e22 + spread, 2.0 * shear * e12)
        current = [ocean * (a + (b - a) * THIRD) for a, b in zip(current, plastic)]
        s11, s22, s12 = current
        pushed = (force(s11, s12), force(s12, s22))
        moving = [scale * (3.0 * moving[i] + fixed[i] + weight * pushed[i]) for i in range(2)]

    for i in range(2):
        o_vel[i] = moving[i][4:8, :COLS]
    for i in range(3):
        o_str[i] = current[i][4:8, :COLS]

    def modes(x):
        total, diff = x + above(x), above(x) - x
        rt, rd = right(total), right(diff)
        w = (0.25 * DT) * ocean
        return w * (total + rt), w * (rt - total), w * (diff + rd), w * (rd - diff)

    def normals(a, b, act):
        mean, half = 0.5 * (a + b), (0.5 * GAUSS) * (b - a)
        return ((5.0 / 9.0) * act * (mean - half), (8.0 / 9.0) * act * mean, (5.0 / 9.0) * act * (mean + half))

    u0, u1, u2, u3 = modes(moving[0])
    v0, v1, v2, v3 = modes(moving[1])
    vn = above(moving[1])
    ue = right(moving[0])
    coefs = [
        3.0 * u0, u1, u2, THIRD * u3,
        3.0 * v0, v1, v2, THIRD * v3,
        5.0 * u0, 5.0 * u1, 2.0 * u1, (5.0 * THIRD) * u2, (5.0 * THIRD) * u3,
        5.0 * v0, 5.0 * v2, 2.0 * v2, (5.0 * THIRD) * v1, (5.0 * THIRD) * v3,
        3.0 * (u2 + v1), 3.0 * v0 + u3, 3.0 * u0 + v3, 1.2 * v1, u1 + v2, 1.2 * u2,
    ]
    coefs += normals(vn, right(vn), (0.25 * DT) * ocean * above(ocean))
    coefs += normals(ue, above(ue), (0.25 * DT) * ocean * right(ocean))
    coefs.append(ocean)
    own_lanes = (at8 // 16) == sublanes((8, 128))
    for i, x in enumerate(coefs):
        kf[i] = x[:, :COLS]
        if i < LAND:
            a, b, c = x[:, :128], x[:, 128:256], x[:, 256:]
            low = turn(jnp.where(at16 >= 124, c, a), 4, 1)
            high = turn(jnp.where(at16 >= 124, b, c), 12, 1)
            z = turn(jnp.where(at16 < 8, low, high), -2, 0)[:8]
            z = jnp.where(own_lanes, pltpu.roll(z, 0, 1, stride=16, stride_axis=0), 0.0)
            for by in (4, 2, 1):
                z = z + turn(z, by, 0)
            ks[i] = z

    arrive(edges)

    reach = []
    for dlat, dlon in AROUND:
        ok = {-1: in_row < 4, 0: (in_row >= 4) & (in_row < 12), 1: in_row >= 12}[dlon]
        reach.append(ok & {-1: at8 < 32, 0: (at8 >= 32) & (at8 < 96), 1: at8 >= 96}[dlat])
    base = []
    for s in range(12):
        strip = st[s]
        for n, (dlat, dlon) in enumerate(AROUND):
            strip = jnp.where(reach[n], turn(lq[n, s // 4], -SLOT[s % 4] + 8 * dlon + 64 * dlat, 1), strip)
        base.append(strip)
    base = (base[:6], base[6:])

    def strip_columns(c):
        e, w = col_traces(c)
        return face_moments([ks[EAST + i] for i in range(3)], e, [turn(x, -1, 1) for x in w])

    def strip_rate(c):
        n, s = row_traces(c)
        north = face_moments([ks[NORTH + i] for i in range(3)], n, [turn(x, -16, 1) for x in s])
        east_m = strip_columns(c)
        g = rate(c, lambda i: ks[VOL + i], north, [turn(x, 16, 1) for x in north], east_m, [turn(x, 1, 1) for x in east_m])
        return g, east_m

    now = base
    rim = []
    for step in range(2):
        got = [strip_rate(c) for c in now]
        rim.append([m for _, m in got])
        if step == 0:
            now = [[a + b for a, b in zip(c, r)] for c, (r, _) in zip(now, got)]
        else:
            now = [
                [0.75 * a + 0.25 * (b + d) for a, b, d in zip(c, f, r)] for c, f, (r, _) in zip(base, now, got)
            ]
    rim.append([strip_columns(c) for c in now])
    for step in range(3):
        for g in range(2):
            for i in range(3):
                sx[step, g, i] = rim[step][g][i]

    lane = lanes((8, COLS))
    both = range(2)

    def six(ref, i, g):
        return [ref[i, g, k] for k in range(6)]

    def spread_row(i):
        return lambda j: jnp.broadcast_to(kf[j, pl.ds(i + 2, 1), :], (8, COLS))

    def open_face(step, i, g, inside, outside, trace):
        k = spread_row(i)
        m = face_moments([k(NORTH + j) for j in range(3)], inside, outside)
        for j in range(3):
            fl[step, g, j] = m[j]
            lo[step, g, j] = trace[j]

    def columns(step, i, g, k, c):
        e, w = col_traces(c)
        m = face_moments([k(EAST + j) for j in range(3)], e, [turn(x, -1, 1) for x in w])
        p = 16 * i
        em, wm = [], []
        for j in range(3):
            r = sx[step, g, j]
            at_east = pltpu.roll(r, lax.rem(127 - 11 - p + 256, 128), 1)
            at_west = pltpu.roll(r, lax.rem(256 - 3 - p, 128), 1)
            x = jnp.where(lane == COLS - 1, jnp.concatenate([at_east, at_east], 1), m[j])
            em.append(x)
            wm.append(jnp.where(lane == 0, jnp.concatenate([at_west, at_west], 1), turn(x, 1, 1)))
        return em, wm

    def wave(w, steps):
        cur, under, old, cols, tops, lows = {}, {}, {}, {}, {}, {}
        last = 1 - jnp.minimum(w, 1)
        k = [spread_row(w + s) for s in range(steps)]
        below_k = [spread_row(w + s - 1) for s in range(steps)]
        for s in range(steps):
            for g in both:
                cur[s, g] = six((c0, c1, c2)[s], w + s, g)
                old[s, g] = cur[s, g] if s == 0 else six(c0, w + s, g)
                tops[s, g] = [fl[s, g, j] for j in range(3)]
                lows[s, g] = [lo[s, g, j] for j in range(3)]
        for g in both:
            n, sth = row_traces(six(c0, jnp.maximum(w - 1, 0), g))
            under[0, g] = ([jnp.where(w == 0, ts[last, g, j], n[j]) for j in range(3)], sth)
        for s in range(steps):
            for g in both:
                cols[s, g] = columns(s, w + s, g, k[s], cur[s, g])
        done = {}
        for s in range(steps):
            for g in both:
                n, sth = under[s, g]
                m = face_moments([below_k[s](NORTH + j) for j in range(3)], n, lows[s, g])
                r = rate(cur[s, g], k[s], tops[s, g], m, *cols[s, g])
                if s == 0:
                    x = [a + b for a, b in zip(cur[s, g], r)]
                elif s == 1:
                    x = [0.75 * a + 0.25 * (b + d) for a, b, d in zip(old[s, g], cur[s, g], r)]
                else:
                    sea = k[s](LAND)
                    x = [sea * (THIRD * a + (2.0 * THIRD) * (b + d)) for a, b, d in zip(old[s, g], cur[s, g], r)]
                done[s, g] = x, m, sth
                if s + 1 < steps:
                    under[s + 1, g] = row_traces(x)
        for s in range(steps):
            for g in both:
                x, m, sth = done[s, g]
                for j in range(3):
                    fl[s, g, j] = m[j]
                    lo[s, g, j] = sth[j]
                for j in range(6):
                    if s < 2:
                        (c1, c2)[s][w + s, g, j] = x[j]
                    else:
                        for t in range(2):
                            o_tr[pl.ds(g * 384 + j * 8 + t * 4 + w, 8, stride=48), :] = x[j][:, t * 128:(t + 1) * 128]

    def run(first_w, count, steps):
        def body(i, _):
            w = first_w - i
            if steps == 3:
                for n, at in enumerate((2, 1, 0)):
                    pl.when(w == at)(functools.partial(arrive, [north_rows[n]]))
            wave(w, steps)
            return 0

        lax.fori_loop(0, count, body, 0)

    arrive(south_rows)
    for g in both:
        n, sth = row_traces(six(c0, 7, g))
        open_face(0, 7, g, n, [tn[g, j] for j in range(3)], sth)
    run(7, 2, 1)
    for g in both:
        n, sth = row_traces(six(c1, 6, g))
        open_face(1, 6, g, n, row_traces(six(c1, 7, g))[1], sth)
    run(5, 2, 2)
    for g in both:
        n, sth = row_traces(six(c2, 5, g))
        open_face(2, 5, g, n, row_traces(six(c2, 6, g))[1], sth)
    run(3, 4, 3)

    sent(first)
    sent(edges)
    sent(north_rows)
    sent(south_rows)


def write_out(a, b, c, out_a, out_b, out_c, sem):
    copies = [pltpu.make_async_copy(x, y, sem.at[i]) for i, (x, y) in enumerate(((a, out_a), (b, out_b), (c, out_c)))]
    for copy in copies:
        copy.start()
    for copy in copies:
        copy.wait()


def local_step(nlat, nlon, tracers, velocity, stress, strength, inverse_mass, wind, ocean_mask):
    linear = tracers.reshape(NTR, 6, ROWS, 2, 128).transpose(0, 1, 3, 2, 4).reshape(768, 128)
    hbm = pl.BlockSpec(memory_space=pltpu.HBM)
    vmem = pl.BlockSpec(memory_space=pltpu.VMEM)
    messages = 8 + 3 + 8 + 6
    shapes = ((2, ROWS, COLS), (3, ROWS, COLS), (768, 128))
    given = [
        pltpu.with_memory_space_constraint(x, pltpu.HBM)
        for x in (linear, velocity, stress, strength, inverse_mass, wind, ocean_mask)
    ]
    results = pl.pallas_call(
        functools.partial(kernel, nlat, nlon),
        out_shape=tuple(pltpu.VMEM(shape, F32) for shape in shapes),
        in_specs=[hbm] * 7,
        out_specs=(vmem, vmem, vmem),
        scratch_shapes=[
            pltpu.VMEM((768, 128), F32),
            pltpu.VMEM((FIELDS, ROWS, COLS), F32),
            pltpu.VMEM((ROWS, COLS), jnp.int32),
            pltpu.VMEM((FIELDS, ROWS, COLS), F32),
            pltpu.VMEM((FIELDS, ROWS, COLS), F32),
            pltpu.VMEM((2, ROWS, COLS), F32),
            pltpu.VMEM((2, 4, 128), F32),
            pltpu.VMEM((2, 4, 2, 4, 128), F32),
            pltpu.VMEM((3, 8, 128), F32),
            pltpu.VMEM((8, 3, 8, 128), F32),
            pltpu.VMEM((8, 2, 6, 8, COLS), F32),
            pltpu.VMEM((2, 2, 3, 8, COLS), F32),
            pltpu.VMEM((2, 3, 8, COLS), F32),
            pltpu.VMEM((2, 3, 8, COLS), F32),
            pltpu.VMEM((2, 3, 8, COLS), F32),
            pltpu.VMEM((8, 2, 6, 8, COLS), F32),
            pltpu.VMEM((8, 2, 6, 8, COLS), F32),
            pltpu.VMEM((COEFS, 16, COLS), F32),
            pltpu.VMEM((LAND, 8, 128), F32),
            pltpu.VMEM((12, 8, 128), F32),
            pltpu.VMEM((3, 2, 3, 8, 128), F32),
            pltpu.VMEM((3, 2, 3, 8, COLS), F32),
            pltpu.VMEM((3, 2, 3, 8, COLS), F32),
            pltpu.SemaphoreType.DMA((8,)),
            pltpu.SemaphoreType.DMA((messages,)),
            pltpu.SemaphoreType.DMA((messages,)),
        ],
        compiler_params=pltpu.CompilerParams(
            collective_id=0, has_side_effects=True, vmem_limit_bytes=16 << 20
        ),
    )(*given)
    new_velocity, new_stress, new_tracers = pl.pallas_call(
        write_out,
        out_shape=tuple(jax.ShapeDtypeStruct(shape, F32) for shape in shapes),
        in_specs=[vmem] * 3,
        out_specs=(hbm, hbm, hbm),
        scratch_shapes=[pltpu.SemaphoreType.DMA((3,))],
        compiler_params=pltpu.CompilerParams(vmem_limit_bytes=16 << 20),
    )(*results)
    new_tracers = new_tracers.reshape(NTR, 6, 2, ROWS, 128).transpose(0, 1, 3, 2, 4).reshape(NTR, 6, ROWS, COLS)
    return new_velocity, new_stress, new_tracers


def solution(mesh):
    in_specs = (
        P(None, None, "lat", "lon"),
        P(None, "lat", "lon"),
        P(None, "lat", "lon"),
        P("lat", "lon"),
        P("lat", "lon"),
        P(None, "lat", "lon"),
        P("lat", "lon"),
    )
    out_specs = (P(None, "lat", "lon"), P(None, "lat", "lon"), P(None, None, "lat", "lon"))
    step = functools.partial(local_step, mesh.shape["lat"], mesh.shape["lon"])
    return jax.shard_map(step, mesh=mesh, in_specs=in_specs, out_specs=out_specs, check_vma=False)
```
